256 devices in a mesh: dp: 32 (over z, x), eig: 2 (over y_lo), tensor: 4 (over y_hi, core).
Axes of the slice: x: 4, y: 4 (y_hi: 2, y_lo: 2; y = y_hi * 2 + y_lo), z: 8, core: 2. Of those that a mesh axis runs over, the one named last changes fastest.
Arguments:
- rotary_queries: bfloat16 [32, 2048, 4096], P('dp', None, ('eig', 'tensor')), may hold values from -180 to 180
- rotary_keys: bfloat16 [32, 2048, 4096], P('dp', None, ('eig', 'tensor')), may hold values from -6 to 6
- value_matrix: bfloat16 [32, 2048, 4096], P('dp', None, ('eig', 'tensor')), may hold values from -6 to 6
- document_index: int32 [32, 2048], P('dp'), may hold values from 0 to 7, never falling along the last dimension, each value on 1 to 1024 neighbouring positions
- cotangent: bfloat16 [32, 2048, 8192], P('dp', None, ('eig', 'tensor')), may hold values from -6 to 6
- adapter_up_weight: bfloat16 [8192, 16], P(('eig', 'tensor')), may hold values from -0.5 to 0.5
- input_eigenvectors: bfloat16 [4096, 4096], P(('eig', 'tensor'), 'dp'), may hold values from -0.09375 to 0.09375
Outputs:
- spectrum: float32 [16, 4096], P(('eig', 'tensor'), 'dp')
The draws below stay inside these ranges and needn't reach their ends.
Inputs may be any that keep to these rules, and one draw needn't show every extreme that they name: `document_index`: document ids never fall along a sequence; each document has 1 to 1024 positions.
All inputs are finite; a program needn't handle non-finite values.
Results may differ from the reference program's by a relative error of at most 0.003.
Values may be sent and summed in bfloat16 or wider, within the bound.
A program may use at most 128 MiB of HBM per device.

```python
import math
import jax
import jax.numpy as jnp
import numpy as np
from jax import lax

MODEL_WIDTH = 8192
HEADS = 32
HEAD_DIM = 128
ADAPTER_RANK = 16
LEN = 2048
DIN = 4096
SEQS = 32


def common_keys(key):
    return jnp.clip(jax.random.normal(key, (SEQS, LEN, DIN), jnp.float32), -6.0, 6.0)


def draw_rotary_keys(key, part):
    shared = common_keys(key)
    return shared.astype(jnp.bfloat16)


def draw_rotary_queries(key, part):
    key = jax.random.fold_in(key, 22)
    fresh = jnp.clip(jax.random.normal(key, (SEQS, LEN, DIN), jnp.float32), -6.0, 6.0)
    return fresh.astype(jnp.bfloat16)


def levels(key, dims, shards, least, top_value):
    def one(axis_at, parts):
        draws = jax.random.uniform(jax.random.fold_in(jax.random.fold_in(key, 6), axis_at), (parts,), jnp.float32, least / len(shards), top_value / len(shards))
        return jnp.repeat(jnp.exp(draws), dims[axis_at] // parts).reshape((-1,) + (1,) * (len(dims) - axis_at - 1))

    gain = one(*shards[0])
    for cut in shards[1:]:
        gain = gain * one(*cut)
    return gain


def length_profile(count, total, bound, lean):
    weights = [(1 << 20) // math.isqrt(grade ** lean) + 1 for grade in range(2, count + 1)]
    rest, counts = total - bound - (count - 1), [1] * (count - 1)
    while rest > 0:
        candidates = [i for i in range(count - 1) if counts[i] < bound]
        mass, remaining = sum([weights[i] for i in candidates]), rest
        for i in candidates:
            extra = min(bound - counts[i], max(1, remaining * weights[i] // mass), rest)
            counts[i] = counts[i] + extra
            rest = rest - extra
    return np.array([bound] + counts)


def uneven_parts(stream_key, count, total, bound, slope):
    if count == 2:
        one = jax.random.randint(stream_key, (), max(1, total - bound), min(bound, total - 1) + 1)
        return jnp.stack([one, total - one])
    sizes = jnp.asarray(length_profile(count, total, bound, slope), jnp.int32)
    twos = (count - 1) // 2
    donor, sink = sizes[1:1 + 2 * twos:2], sizes[2:2 + 2 * twos:2]
    slack = jnp.minimum(donor - 1, bound - sink)
    moved = jax.random.randint(jax.random.fold_in(stream_key, 1), (twos,), 0, 1 << 20) % (slack + 1)
    sizes = sizes.at[1:1 + 2 * twos:2].set(donor - moved).at[2:2 + 2 * twos:2].set(sink + moved)
    return sizes[jax.random.permutation(jax.random.fold_in(stream_key, 2), count)]


def gaussian(stream_key, dims, spread, bound, shards=(), kind=jnp.bfloat16):
    array = jax.random.normal(stream_key, dims, jnp.float32) * spread
    if len(shards) > 0:
        array = levels(stream_key, dims, shards, -0.22, 0.18) * array
    return jnp.clip(array, min=-bound, max=bound).astype(kind)


def setup_inputs(seed: int = 0) -> dict:
    key_of = jax.random.split(jax.random.key(seed), 8)
    rotary_queries = draw_rotary_queries(jax.random.fold_in(key_of[7], 71), 0)
    rotary_keys = draw_rotary_keys(jax.random.fold_in(key_of[7], 71), 0)
    value_matrix = gaussian(key_of[2], (SEQS, LEN, DIN), 1.0, 6.0, ((0, 32), (2, 8)))
    document_index = jax.vmap(lambda own: jnp.searchsorted(jnp.cumsum(uneven_parts(own, 8, LEN, LEN // 2, 2)), jnp.arange(LEN), side="right"))(jax.random.split(key_of[3], SEQS)).reshape((SEQS, LEN)).astype(jnp.int32)
    cotangent = gaussian(key_of[4], (SEQS, LEN, MODEL_WIDTH), 1.0, 6.0, ((0, 32), (2, 8)))
    adapter_up_weight = gaussian(key_of[5], (MODEL_WIDTH, ADAPTER_RANK), (MODEL_WIDTH // 64) ** -0.5, 0.5, ((0, 8),))
    input_eigenvectors = gaussian(key_of[6], (DIN, DIN), DIN ** -0.5, 0.09375, ((0, 8), (1, 32)))
    return {"rotary_queries": rotary_queries, "rotary_keys": rotary_keys, "value_matrix": value_matrix, "document_index": document_index, "cotangent": cotangent, "adapter_up_weight": adapter_up_weight, "input_eigenvectors": input_eigenvectors}


def head_attention(query, key_part, value_part, allowed):
    scores = jnp.dot(query, key_part.T, preferred_element_type=jnp.float32) * (HEAD_DIM ** -0.5)
    scores = jnp.where(allowed, scores, -1e30)
    row_max = jnp.max(scores, axis=-1, keepdims=True)
    expon = jnp.exp(scores - row_max)
    row_total = jnp.sum(expon, axis=-1, keepdims=True)
    weights = (expon / row_total).astype(jnp.bfloat16)
    return jnp.dot(weights, value_part, preferred_element_type=jnp.float32).astype(jnp.bfloat16)


def reference(rotary_queries, rotary_keys, value_matrix, document_index, cotangent, adapter_up_weight, input_eigenvectors):
    def one_sequence(items):
        query, key_part, value_part, document, incoming_gradient = items
        position = jnp.arange(LEN)
        allowed = (document[:, None] == document[None, :]) & (position[None, :] <= position[:, None])
        split_q = query.reshape(LEN, HEADS, HEAD_DIM).transpose(1, 0, 2)
        split_k = key_part.reshape(LEN, HEADS, HEAD_DIM).transpose(1, 0, 2)
        split_v = value_part.reshape(LEN, HEADS, HEAD_DIM).transpose(1, 0, 2)
        heads_out = lax.map(lambda trio: head_attention(trio[0], trio[1], trio[2], allowed), (split_q, split_k, split_v))
        mixed = heads_out.transpose(1, 0, 2).reshape(LEN, DIN)
        reduced_rank = jnp.dot(incoming_gradient, adapter_up_weight, preferred_element_type=jnp.float32).astype(jnp.bfloat16)
        grad = (jnp.dot(reduced_rank.T, mixed, preferred_element_type=jnp.float32) * (LEN ** -0.5)).astype(jnp.bfloat16)
        rotated = jnp.dot(grad, input_eigenvectors, preferred_element_type=jnp.float32)
        return rotated * rotated

    squares = lax.map(one_sequence, (rotary_queries, rotary_keys, value_matrix, document_index, cotangent))
    return jnp.sum(squares, axis=0) / SEQS
```

```python
import math

import jax
import jax.numpy as jnp
from jax import lax
from jax.experimental import pallas as pl
from jax.experimental.pallas import tpu as pltpu
from jax.sharding import PartitionSpec as P

HEAD_DIM = 128
HEADS = 4
LEN = 2048
RANK = 16
COLS = HEADS * HEAD_DIM
FEATURES = 1024
SEQS = 32
WINDOW = 1024
BLOCK = 256
BLOCKS = LEN // BLOCK
SCALE = math.log2(math.e) / math.sqrt(HEAD_DIM)
HALF = LEN // 2
NEG = -1e30
MESH = pl.DeviceIdType.MESH
f32 = jnp.float32
bf16 = jnp.bfloat16


def dot(a, b, ca=1, cb=0):
    return lax.dot_general(a, b, (((ca,), (cb,)), ((), ())), preferred_element_type=f32)


def places():
    dp = lax.axis_index("dp")
    eig = lax.axis_index("eig")
    tensor = lax.axis_index("tensor")
    return dp // 4, lax.rem(dp, 4), 2 * (tensor // 2) + eig, lax.rem(tensor, 2)


def device(z, x, y, core):
    return {"dp": 4 * z + x, "eig": lax.rem(y, 2), "tensor": 2 * (y // 2) + core}


def kernel(
    q_hbm, k_hbm, v_hbm, doc_hbm, cot_hbm, up_hbm, vec_hbm, out_ref,
    q, k, v, doc, cot, up, vec, kx, qx, perm, mixed,
    low_part, low_core, low_send, low_y, low,
    grads, part, part_core, rot_send, rot_y, spec_send, spec_x,
    in_sem, cot_sem, sc_send, sc_recv, sy_send, sy_recv, sx_send, sx_recv, sz_send, sz_recv,
):
    z, x, y, core = places()
    other = device(z, x, y, 1 - core)
    y_to = [device(z, x, lax.rem(y + d, 4), core) for d in range(1, 4)]
    x_to = [device(z, lax.rem(x + d, 4), y, core) for d in range(1, 4)]
    x_from = [device(z, lax.rem(x + 4 - d, 4), y, core) for d in range(1, 4)]
    z_to = [device(lax.rem(z + d, 8), x, y, core) for d in range(1, 8)]
    peers = [other] + y_to + x_to + z_to

    def remote(src, dst, send, recv, to):
        return pltpu.make_async_remote_copy(
            src_ref=src, dst_ref=dst, send_sem=send, recv_sem=recv, device_id=to, device_id_type=MESH
        )

    barrier = pltpu.get_barrier_semaphore()
    for peer in peers:
        pl.semaphore_signal(barrier, inc=1, device_id=peer, device_id_type=MESH)

    loads = [
        pltpu.make_async_copy(src, dst, in_sem.at[n])
        for n, (src, dst) in enumerate(
            [
                (up_hbm, up),
                (doc_hbm, doc),
                (q_hbm.at[0], q),
                (k_hbm.at[0], k),
                (v_hbm.at[0], v),
                (vec_hbm, vec.at[0]),
            ]
        )
    ]
    chunks = [
        pltpu.make_async_copy(
            cot_hbm.at[0, pl.ds(512 * c, 512), :], cot.at[pl.ds(512 * c, 512), :], cot_sem.at[c]
        )
        for c in range(4)
    ]
    loads[0].start()
    loads[1].start()
    for c in chunks:
        c.start()
    for c in loads[2:]:
        c.start()

    loads[1].wait()
    one_hot = jnp.where(
        lax.broadcasted_iota(jnp.int32, (HEAD_DIM, LEN), 0) == doc[...], 1.0, 0.0
    ).astype(f32)
    turned = one_hot.T
    kx[...] = turned.astype(bf16)
    qx[...] = jnp.where(turned > 0.5, 0.0, NEG).astype(bf16)
    row = lax.broadcasted_iota(jnp.int32, (128, 128), 0)
    source = (
        16 * ((row >> 1) & 7) + 8 * ((row >> 4) & 1) + 4 * ((row >> 5) & 1) + 2 * (row >> 6) + (row & 1)
    )
    perm[...] = jnp.where(lax.broadcasted_iota(jnp.int32, (128, 128), 1) == source, 1.0, 0.0).astype(bf16)

    loads[0].wait()
    up_t = up[...].astype(f32).T.astype(bf16)
    for c in range(4):
        chunks[c].wait()
        low_part[c // 2, :, pl.ds(512 * (c % 2), 512)] = dot(
            up_t, cot[512 * c : 512 * (c + 1), :], 1, 1
        )
    for c in loads[2:]:
        c.wait()

    lower = lax.broadcasted_iota(jnp.int32, (BLOCK, BLOCK), 1) <= lax.broadcasted_iota(
        jnp.int32, (BLOCK, BLOCK), 0
    )
    ones = jnp.ones((BLOCK, HEAD_DIM), bf16)

    def scores(h, i):
        hs = slice(h * HEAD_DIM, (h + 1) * HEAD_DIM)
        rows = slice(i * BLOCK, (i + 1) * BLOCK)
        first = max(0, (i * BLOCK - WINDOW + 1) // BLOCK)
        query = jnp.concatenate([q[rows, hs], qx[rows, :]], axis=1)
        result = []
        for j in range(first, i + 1):
            at = slice(j * BLOCK, (j + 1) * BLOCK)
            key = jnp.concatenate([k[at, hs], kx[at, :]], axis=1)
            s = dot(query, key, 1, 1)
            result.append(jnp.where(lower, s, NEG) if j == i else s)
        return first, result

    def mix(h, i, first, blocks):
        hs = slice(h * HEAD_DIM, (h + 1) * HEAD_DIM)
        top = blocks[0]
        for s in blocks[1:]:
            top = jnp.maximum(top, s)
        top = jnp.max(top, axis=1, keepdims=True)
        total = None
        for n, s in enumerate(blocks):
            at = slice((first + n) * BLOCK, (first + n + 1) * BLOCK)
            weights = jnp.exp2((s - top) * SCALE).astype(bf16)
            term = dot(weights, jnp.concatenate([v[at, hs], ones], axis=1))
            total = term if total is None else total + term
        mixed[i * BLOCK : (i + 1) * BLOCK, hs] = (
            total[:, :HEAD_DIM] / total[:, HEAD_DIM:]
        ).astype(bf16)

    sent = []

    def send_low_core():
        pl.semaphore_wait(barrier, len(peers))
        c = remote(low_part.at[1 - core], low_core, sc_send.at[0], sc_recv.at[0], other)
        c.start()
        sent.append(c)
        for d in range(1, 4):
            e = remote(vec.at[0], vec.at[d], sx_send.at[d - 1], sx_recv.at[d - 1], x_to[d - 1])
            e.start()
            sent.append(e)

    def send_low_y():
        sent[0].wait_recv()
        mine = low_part[core] + low_core[...]
        low_part[core] = mine
        low_send[...] = mine.astype(bf16)
        for d in range(1, 4):
            c = remote(low_send, low_y.at[d - 1], sy_send.at[d - 1], sy_recv.at[d - 1], y_to[d - 1])
            c.start()
            sent.append(c)

    def send_low_back():
        total = low_part[core]
        for d in range(1, 4):
            sent[3 + d].wait_recv()
            total = total + low_y[d - 1].astype(f32)
        low[core] = total.astype(bf16)
        c = remote(low.at[core], low.at[core], sc_send.at[1], sc_recv.at[1], other)
        c.start()
        sent.append(c)

    steps = {STEP_CORE: send_low_core, STEP_Y: send_low_y, STEP_BACK: send_low_back}
    units = [(h, i) for h in range(HEADS) for i in range(BLOCKS)]
    held = None
    for n, (h, i) in enumerate(units):
        ready = scores(h, i)
        if held is not None:
            mix(*held)
        held = (h, i, *ready)
        if n in steps:
            steps[n]()
    mix(*held)

    sent[7].wait_recv()
    grad = dot(low[0], mixed[:HALF, :]) + dot(low[1], mixed[HALF:, :])
    grads[0] = (grad * LEN ** (-0.5)).astype(bf16)
    sent_z = []
    for d in range(7, 0, -1):
        c = remote(grads.at[0], grads.at[d], sz_send.at[d - 1], sz_recv.at[d - 1], z_to[d - 1])
        c.start()
        sent_z.append(c)
    for c in sent[1:4]:
        c.wait_recv()
    columns = jnp.concatenate([vec[d] for d in range(4)], axis=1)
    for c in sent_z:
        c.wait_recv()

    ordered = dot(perm[...], grads[...].reshape(8 * RANK, COLS)).astype(bf16)
    part[...] = dot(ordered, columns).reshape(2, 64, 512)
    c = remote(part.at[1 - core], part_core, sc_send.at[2], sc_recv.at[2], other)
    c.start()
    c.wait_recv()
    sent.append(c)
    part[core] = part[core] + part_core[...]
    rot_send[...] = part[core].reshape(4, 16, 512).astype(bf16)
    sent_y = []
    for d in range(1, 4):
        c = remote(
            rot_send.at[lax.rem(y + d, 4)], rot_y.at[d - 1], sy_send.at[2 + d], sy_recv.at[2 + d], y_to[d - 1]
        )
        c.start()
        sent_y.append(c)
    rotated = part[core, pl.ds(pl.multiple_of(16 * y, 16), 16), :]
    for d, c in enumerate(sent_y):
        c.wait_recv()
        rotated = rotated + rot_y[d].astype(f32)
    squares = rotated * rotated
    pairs = squares[:8] + squares[8:]
    pairs = pairs + pltpu.roll(pairs, 4, 0)
    pairs = pairs + pltpu.roll(pairs, 2, 0)
    for d in range(4):
        spec_send[d] = pairs[:, 128 * d : 128 * (d + 1)]
    sent_x = []
    for d in range(1, 4):
        c = remote(spec_send.at[d], spec_x.at[d - 1], sx_send.at[2 + d], sx_recv.at[2 + d], x_from[d - 1])
        c.start()
        sent_x.append(c)
    total = spec_send[0]
    for d, c in enumerate(sent_x):
        c.wait_recv()
        total = total + spec_x[d]
    out_ref[...] = total[:2]
    for c in sent + sent_z + sent_y + sent_x:
        c.wait_send()


STEP_CORE, STEP_Y, STEP_BACK = 19, 22, 30


def shards(queries, keys, values, documents, cotangent, up, vectors):
    vmem = pltpu.VMEM
    dma = pltpu.SemaphoreType.DMA
    summed = pl.pallas_call(
        kernel,
        out_shape=jax.ShapeDtypeStruct((2, 128), f32),
        in_specs=[pl.BlockSpec(memory_space=pl.ANY)] * 7,
        out_specs=pl.BlockSpec(memory_space=pltpu.VMEM),
        scratch_shapes=[
            vmem((LEN, COLS), bf16),
            vmem((LEN, COLS), bf16),
            vmem((LEN, COLS), bf16),
            vmem((1, LEN), jnp.int32),
            vmem((LEN, FEATURES), bf16),
            vmem((FEATURES, RANK), bf16),
            vmem((4, COLS, 128), bf16),
            vmem((LEN, HEAD_DIM), bf16),
            vmem((LEN, HEAD_DIM), bf16),
            vmem((128, 128), bf16),
            vmem((LEN, COLS), bf16),
            vmem((2, RANK, HALF), f32),
            vmem((RANK, HALF), f32),
            vmem((RANK, HALF), bf16),
            vmem((3, RANK, HALF), bf16),
            vmem((2, RANK, HALF), bf16),
            vmem((8, RANK, COLS), bf16),
            vmem((2, 64, 512), f32),
            vmem((64, 512), f32),
            vmem((4, 16, 512), bf16),
            vmem((3, 16, 512), bf16),
            vmem((4, 8, 128), f32),
            vmem((3, 8, 128), f32),
            dma((6,)),
            dma((4,)),
            dma((3,)),
            dma((3,)),
            dma((6,)),
            dma((6,)),
            dma((6,)),
            dma((6,)),
            dma((7,)),
            dma((7,)),
        ],
        compiler_params=pltpu.CompilerParams(
            collective_id=0, has_side_effects=True, vmem_limit_bytes=56 * 2**20
        ),
    )(queries, keys, values, documents, cotangent, up, vectors)
    return summed * (1.0 / SEQS)


def solution(mesh):
    return jax.shard_map(
        shards,
        mesh=mesh,
        in_specs=(
            P("dp", None, ("eig", "tensor")),
            P("dp", None, ("eig", "tensor")),
            P("dp", None, ("eig", "tensor")),
            P("dp", None),
            P("dp", None, ("eig", "tensor")),
            P(("eig", "tensor"), None),
            P(("eig", "tensor"), "dp"),
        ),
        out_specs=P(("eig", "tensor"), "dp"),
        check_vma=False,
    )
```

```python
import math

import jax
import jax.numpy as jnp
from jax import lax
from jax.experimental import pallas as pl
from jax.experimental.pallas import tpu as pltpu
from jax.sharding import PartitionSpec as P

HEAD_DIM = 128
HEADS = 4
LEN = 2048
RANK = 16
COLS = HEADS * HEAD_DIM
FEATURES = 1024
SEQS = 32
WINDOW = 1024
BLOCK = 256
BLOCKS = LEN // BLOCK
SCALE = math.log2(math.e) / math.sqrt(HEAD_DIM)
HALF = LEN // 2
NEG = -1e30
MESH = pl.DeviceIdType.MESH
f32 = jnp.float32
bf16 = jnp.bfloat16


def dot(a, b, ca=1, cb=0):
    return lax.dot_general(a, b, (((ca,), (cb,)), ((), ())), preferred_element_type=f32)


def places():
    dp = lax.axis_index("dp")
    eig = lax.axis_index("eig")
    tensor = lax.axis_index("tensor")
    return dp // 4, lax.rem(dp, 4), 2 * (tensor // 2) + eig, lax.rem(tensor, 2)


def device(z, x, y, core):
    return {"dp": 4 * z + x, "eig": lax.rem(y, 2), "tensor": 2 * (y // 2) + core}


def kernel(
    q_hbm, k_hbm, v_hbm, doc_hbm, cot_hbm, up_hbm, vec_hbm, out_ref,
    q, k, v, doc, cot, up, vec, kx, qx, perm, mixed,
    low_part, low_core, low_send, low_y, low,
    grads, part, part_core, rot_send, rot_y, spec_send, spec_x,
    in_sem, cot_sem, row_sem, sc_send, sc_recv, sy_send, sy_recv, sx_send, sx_recv, sz_send, sz_recv,
):
    z, x, y, core = places()
    other = device(z, x, y, 1 - core)
    y_to = [device(z, x, lax.rem(y + d, 4), core) for d in range(1, 4)]
    x_to = [device(z, lax.rem(x + d, 4), y, core) for d in range(1, 4)]
    x_from = [device(z, lax.rem(x + 4 - d, 4), y, core) for d in range(1, 4)]
    z_to = [device(lax.rem(z + d, 8), x, y, core) for d in range(1, 8)]
    peers = [other] + y_to + x_to + z_to

    def remote(src, dst, send, recv, to):
        return pltpu.make_async_remote_copy(
            src_ref=src, dst_ref=dst, send_sem=send, recv_sem=recv, device_id=to, device_id_type=MESH
        )

    barrier = pltpu.get_barrier_semaphore()
    for peer in peers:
        pl.semaphore_signal(barrier, inc=1, device_id=peer, device_id_type=MESH)

    loads = [
        pltpu.make_async_copy(src, dst, in_sem.at[n])
        for n, (src, dst) in enumerate([(doc_hbm, doc), (vec_hbm, vec.at[0]), (up_hbm, up)])
    ]
    row_loads = []
    for n in range(2):
        at = pl.ds(512 if n else 0, 1536 if n else 512)
        for m, (src, dst) in enumerate([(k_hbm, k), (q_hbm, q), (v_hbm, v)]):
            row_loads.append(pltpu.make_async_copy(src.at[0, at, :], dst.at[at, :], row_sem.at[3 * n + m]))
    chunks = [
        pltpu.make_async_copy(
            cot_hbm.at[0, pl.ds(512 * c, 512), :], cot.at[pl.ds(512 * c, 512), :], cot_sem.at[c]
        )
        for c in range(4)
    ]
    for c in loads + row_loads[:3]:
        c.start()

    loads[0].wait()
    one_hot = jnp.where(
        lax.broadcasted_iota(jnp.int32, (HEAD_DIM, LEN), 0) == doc[...], 1.0, 0.0
    ).astype(f32)
    turned = one_hot.T
    kx[...] = turned.astype(bf16)
    qx[...] = jnp.where(turned > 0.5, 0.0, NEG).astype(bf16)
    row = lax.broadcasted_iota(jnp.int32, (128, 128), 0)
    source = (
        16 * ((row >> 1) & 7) + 8 * ((row >> 4) & 1) + 4 * ((row >> 5) & 1) + 2 * (row >> 6) + (row & 1)
    )
    perm[...] = jnp.where(lax.broadcasted_iota(jnp.int32, (128, 128), 1) == source, 1.0, 0.0).astype(bf16)

    lower = lax.broadcasted_iota(jnp.int32, (BLOCK, BLOCK), 1) <= lax.broadcasted_iota(
        jnp.int32, (BLOCK, BLOCK), 0
    )
    ones = jnp.ones((BLOCK, HEAD_DIM), bf16)

    def scores(h, i):
        hs = slice(h * HEAD_DIM, (h + 1) * HEAD_DIM)
        rows = slice(i * BLOCK, (i + 1) * BLOCK)
        first = max(0, (i * BLOCK - WINDOW + 1) // BLOCK)
        query = jnp.concatenate([q[rows, hs], qx[rows, :]], axis=1)
        result = []
        for j in range(first, i + 1):
            at = slice(j * BLOCK, (j + 1) * BLOCK)
            key = jnp.concatenate([k[at, hs], kx[at, :]], axis=1)
            s = dot(query, key, 1, 1)
            result.append(jnp.where(lower, s, NEG) if j == i else s)
        return first, result

    def mix(h, i, first, blocks):
        hs = slice(h * HEAD_DIM, (h + 1) * HEAD_DIM)
        top = blocks[0]
        for s in blocks[1:]:
            top = jnp.maximum(top, s)
        top = jnp.max(top, axis=1, keepdims=True)
        total = None
        for n, s in enumerate(blocks):
            at = slice((first + n) * BLOCK, (first + n + 1) * BLOCK)
            weights = jnp.exp2((s - top) * SCALE).astype(bf16)
            term = dot(weights, jnp.concatenate([v[at, hs], ones], axis=1))
            total = term if total is None else total + term
        mixed[i * BLOCK : (i + 1) * BLOCK, hs] = (
            total[:, :HEAD_DIM] / total[:, HEAD_DIM:]
        ).astype(bf16)

    sent = []

    def project():
        loads[2].wait()
        for c in range(4):
            chunks[c].wait()
            if c == 1:
                for load in row_loads[3:]:
                    load.start()
            low_part[c // 2, :, pl.ds(512 * (c % 2), 512)] = dot(
                up[...], cot[512 * c : 512 * (c + 1), :], 1, 1
            )
        loads[1].wait()
        for c in row_loads[3:]:
            c.wait()

    def send_low_core():
        pl.semaphore_wait(barrier, len(peers))
        c = remote(low_part.at[1 - core], low_core, sc_send.at[0], sc_recv.at[0], other)
        c.start()
        sent.append(c)

    def send_low_y():
        sent[0].wait_recv()
        mine = low_part[core] + low_core[...]
        low_part[core] = mine
        low_send[...] = mine.astype(bf16)
        for d in range(1, 4):
            c = remote(low_send, low_y.at[d - 1], sy_send.at[d - 1], sy_recv.at[d - 1], y_to[d - 1])
            c.start()
            sent.append(c)
        for d in range(1, 4):
            c = remote(vec.at[0], vec.at[d], sx_send.at[d - 1], sx_recv.at[d - 1], x_to[d - 1])
            c.start()
            sent.append(c)

    def send_low_back():
        total = low_part[core]
        for d in range(1, 4):
            sent[d].wait_recv()
            total = total + low_y[d - 1].astype(f32)
        low[core] = total.astype(bf16)
        c = remote(low.at[core], low.at[core], sc_send.at[1], sc_recv.at[1], other)
        c.start()
        sent.append(c)

    def early_gradient():
        sent[7].wait_recv()
        send_gradient(0)

    sent_z = []

    def send_gradient(n):
        hs = slice(0, 384) if n == 0 else slice(384, 512)
        grad = dot(low[0], mixed[:HALF, hs]) + dot(low[1], mixed[HALF:, hs])
        grads[0, :, hs] = (grad * LEN ** (-0.5)).astype(bf16)
        for d in range(7, 0, -1):
            at = 7 * n + d - 1
            c = remote(
                grads.at[0, :, pl.ds(384 * n, 128 if n else 384)],
                grads.at[d, :, pl.ds(384 * n, 128 if n else 384)],
                sz_send.at[at],
                sz_recv.at[at],
                z_to[d - 1],
            )
            c.start()
            sent_z.append(c)

    units = [(h, i) for h in range(HEADS) for i in range(2)]
    units += [(h, i) for h in range(HEADS) for i in range(2, BLOCKS)]
    events = [(12, project), (PLAN[0], send_low_core), (PLAN[1], send_low_y), (PLAN[2], send_low_back)]
    events.append((PLAN[3], early_gradient))
    done = 0
    for c in row_loads[:3]:
        c.wait()
    for c in chunks:
        c.start()
    held = None
    for h, i in units:
        ready = scores(h, i)
        if held is not None:
            mix(*held)
        held = (h, i, *ready)
        done += len(ready[1])
        while events and events[0][0] <= done:
            events.pop(0)[1]()
    mix(*held)

    send_gradient(1)
    for c in sent[4:7]:
        c.wait_recv()
    columns = jnp.concatenate([vec[d] for d in range(4)], axis=1)
    for c in sent_z:
        c.wait_recv()

    ordered = dot(perm[...], grads[...].reshape(8 * RANK, COLS)).astype(bf16)
    part[...] = dot(ordered, columns).reshape(2, 64, 512)
    c = remote(part.at[1 - core], part_core, sc_send.at[2], sc_recv.at[2], other)
    c.start()
    c.wait_recv()
    sent.append(c)
    part[core] = part[core] + part_core[...]
    rot_send[...] = part[core].reshape(4, 16, 512).astype(bf16)
    sent_y = []
    for d in range(1, 4):
        c = remote(
            rot_send.at[lax.rem(y + d, 4)], rot_y.at[d - 1], sy_send.at[2 + d], sy_recv.at[2 + d], y_to[d - 1]
        )
        c.start()
        sent_y.append(c)
    rotated = part[core, pl.ds(pl.multiple_of(16 * y, 16), 16), :]
    for d, c in enumerate(sent_y):
        c.wait_recv()
        rotated = rotated + rot_y[d].astype(f32)
    squares = rotated * rotated
    pairs = squares[:8] + squares[8:]
    pairs = pairs + pltpu.roll(pairs, 4, 0)
    pairs = pairs + pltpu.roll(pairs, 2, 0)
    for d in range(4):
        spec_send[d] = pairs[:, 128 * d : 128 * (d + 1)]
    sent_x = []
    for d in range(1, 4):
        c = remote(spec_send.at[d], spec_x.at[d - 1], sx_send.at[2 + d], sx_recv.at[2 + d], x_from[d - 1])
        c.start()
        sent_x.append(c)
    total = spec_send[0]
    for d, c in enumerate(sent_x):
        c.wait_recv()
        total = total + spec_x[d]
    out_ref[...] = total[:2]
    for c in sent + sent_z + sent_y + sent_x:
        c.wait_send()


PLAN = (20, 34, 92, 108)


def shards(queries, keys, values, documents, cotangent, up, vectors):
    vmem = pltpu.VMEM
    dma = pltpu.SemaphoreType.DMA
    summed = pl.pallas_call(
        kernel,
        out_shape=jax.ShapeDtypeStruct((2, 128), f32),
        in_specs=[pl.BlockSpec(memory_space=pl.ANY)] * 7,
        out_specs=pl.BlockSpec(memory_space=pltpu.VMEM),
        scratch_shapes=[
            vmem((LEN, COLS), bf16),
            vmem((LEN, COLS), bf16),
            vmem((LEN, COLS), bf16),
            vmem((1, LEN), jnp.int32),
            vmem((LEN, FEATURES), bf16),
            vmem((RANK, FEATURES), bf16),
            vmem((4, COLS, 128), bf16),
            vmem((LEN, HEAD_DIM), bf16),
            vmem((LEN, HEAD_DIM), bf16),
            vmem((128, 128), bf16),
            vmem((LEN, COLS), bf16),
            vmem((2, RANK, HALF), f32),
            vmem((RANK, HALF), f32),
            vmem((RANK, HALF), bf16),
            vmem((3, RANK, HALF), bf16),
            vmem((2, RANK, HALF), bf16),
            vmem((8, RANK, COLS), bf16),
            vmem((2, 64, 512), f32),
            vmem((64, 512), f32),
            vmem((4, 16, 512), bf16),
            vmem((3, 16, 512), bf16),
            vmem((4, 8, 128), f32),
            vmem((3, 8, 128), f32),
            dma((3,)),
            dma((4,)),
            dma((6,)),
            dma((3,)),
            dma((3,)),
            dma((6,)),
            dma((6,)),
            dma((6,)),
            dma((6,)),
            dma((14,)),
            dma((14,)),
        ],
        compiler_params=pltpu.CompilerParams(
            collective_id=0, has_side_effects=True, vmem_limit_bytes=56 * 2**20
        ),
    )(queries, keys, values, documents, cotangent, up.T, vectors)
    return summed * (1.0 / SEQS)


def solution(mesh):
    return jax.shard_map(
        shards,
        mesh=mesh,
        in_specs=(
            P("dp", None, ("eig", "tensor")),
            P("dp", None, ("eig", "tensor")),
            P("dp", None, ("eig", "tensor")),
            P("dp", None),
            P("dp", None, ("eig", "tensor")),
            P(("eig", "tensor"), None),
            P(("eig", "tensor"), "dp"),
        ),
        out_specs=P(("eig", "tensor"), "dp"),
        check_vma=False,
    )
```

```python
import math

import jax
import jax.numpy as jnp
from jax import lax
from jax.experimental import pallas as pl
from jax.experimental.pallas import tpu as pltpu
from jax.sharding import PartitionSpec as P

HEAD_DIM = 128
HEADS = 4
LEN = 2048
RANK = 16
COLS = HEADS * HEAD_DIM
FEATURES = 1024
SEQS = 32
WINDOW = 1024
BLOCK = 256
BLOCKS = LEN // BLOCK
SCALE = math.log2(math.e) / math.sqrt(HEAD_DIM)
HALF = LEN // 2
NEG = -1e30
MESH = pl.DeviceIdType.MESH
f32 = jnp.float32
bf16 = jnp.bfloat16


def dot(a, b, ca=1, cb=0):
    return lax.dot_general(a, b, (((ca,), (cb,)), ((), ())), preferred_element_type=f32)


def places():
    dp = lax.axis_index("dp")
    eig = lax.axis_index("eig")
    tensor = lax.axis_index("tensor")
    return dp // 4, lax.rem(dp, 4), 2 * (tensor // 2) + eig, lax.rem(tensor, 2)


def device(z, x, y, core):
    return {"dp": 4 * z + x, "eig": lax.rem(y, 2), "tensor": 2 * (y // 2) + core}


def kernel(
    q_hbm, k_hbm, v_hbm, doc_hbm, cot_hbm, up_hbm, vec_hbm, out_ref,
    q, k, v, doc, cot, up, vec, kx, qx, whole, mixed,
    low_part, low_core, low_send, low_y, low,
    grads, part, part_core, rot_send, rot_y, spec_send, spec_x,
    in_sem, cot_sem, row_sem, sc_send, sc_recv, sy_send, sy_recv, sx_send, sx_recv, sz_send, sz_recv,
):
    z, x, y, core = places()
    other = device(z, x, y, 1 - core)
    y_to = [device(z, x, lax.rem(y + d, 4), core) for d in range(1, 4)]
    x_to = [device(z, lax.rem(x + d, 4), y, core) for d in range(1, 4)]
    x_from = [device(z, lax.rem(x + 4 - d, 4), y, core) for d in range(1, 4)]
    z_to = [device(lax.rem(z + d, 8), x, y, core) for d in range(1, 8)]
    peers = [other] + y_to + x_to + z_to

    def remote(src, dst, send, recv, to):
        return pltpu.make_async_remote_copy(
            src_ref=src, dst_ref=dst, send_sem=send, recv_sem=recv, device_id=to, device_id_type=MESH
        )

    loads = [
        pltpu.make_async_copy(src, dst, in_sem.at[n])
        for n, (src, dst) in enumerate([(doc_hbm, doc), (vec_hbm, vec.at[0]), (up_hbm, up)])
    ]
    row_loads = []
    for n in range(2):
        at = pl.ds(512 if n else 0, 1536 if n else 512)
        for m, (src, dst) in enumerate([(k_hbm, k), (q_hbm, q), (v_hbm, v)]):
            row_loads.append(pltpu.make_async_copy(src.at[0, at, :], dst.at[at, :], row_sem.at[3 * n + m]))
    chunks = [
        pltpu.make_async_copy(
            cot_hbm.at[0, pl.ds(512 * c, 512), :], cot.at[pl.ds(512 * c, 512), :], cot_sem.at[c]
        )
        for c in range(4)
    ]
    for c in row_loads[:3] + loads + chunks[:1]:
        c.start()
    barrier = pltpu.get_barrier_semaphore()
    for peer in peers:
        pl.semaphore_signal(barrier, inc=1, device_id=peer, device_id_type=MESH)

    loads[0].wait()
    one_hot = jnp.where(
        lax.broadcasted_iota(jnp.int32, (HEAD_DIM, LEN), 0) == doc[...], 1.0, 0.0
    ).astype(f32)
    turned = one_hot.T
    kx[...] = turned.astype(bf16)
    qx[...] = jnp.where(turned > 0.5, 0.0, NEG).astype(bf16)
    lower = lax.broadcasted_iota(jnp.int32, (BLOCK, BLOCK), 1) <= lax.broadcasted_iota(
        jnp.int32, (BLOCK, BLOCK), 0
    )
    ones = jnp.ones((BLOCK, HEAD_DIM), bf16)

    def scores(h, i):
        hs = slice(h * HEAD_DIM, (h + 1) * HEAD_DIM)
        rows = slice(i * BLOCK, (i + 1) * BLOCK)
        first = max(0, (i * BLOCK - WINDOW + 1) // BLOCK)
        query = jnp.concatenate([q[rows, hs], qx[rows, :]], axis=1)
        result = []
        for j in range(first, i + 1):
            at = slice(j * BLOCK, (j + 1) * BLOCK)
            key = jnp.concatenate([k[at, hs], kx[at, :]], axis=1)
            s = dot(query, key, 1, 1)
            result.append(jnp.where(lower, s, NEG) if j == i else s)
        return first, result

    def mix(h, i, first, blocks):
        hs = slice(h * HEAD_DIM, (h + 1) * HEAD_DIM)
        top = blocks[0]
        for s in blocks[1:]:
            top = jnp.maximum(top, s)
        top = jnp.max(top, axis=1, keepdims=True)
        total = None
        for n, s in enumerate(blocks):
            at = slice((first + n) * BLOCK, (first + n + 1) * BLOCK)
            weights = jnp.exp2((s - top) * SCALE).astype(bf16)
            term = dot(weights, jnp.concatenate([v[at, hs], ones], axis=1))
            total = term if total is None else total + term
        mixed[i * BLOCK : (i + 1) * BLOCK, hs] = (
            total[:, :HEAD_DIM] / total[:, HEAD_DIM:]
        ).astype(bf16)

    sent = []

    def project():
        loads[2].wait()
        for c in range(4):
            chunks[c].wait()
            if c == 0:
                for load in row_loads[3:]:
                    load.start()
            low_part[c // 2, :, pl.ds(512 * (c % 2), 512)] = dot(
                up[...], cot[512 * c : 512 * (c + 1), :], 1, 1
            )
        loads[1].wait()
        for c in row_loads[3:]:
            c.wait()

    def send_low_core():
        pl.semaphore_wait(barrier, len(peers))
        c = remote(low_part.at[1 - core], low_core, sc_send.at[0], sc_recv.at[0], other)
        c.start()
        sent.append(c)

    def send_low_y():
        sent[0].wait_recv()
        mine = low_part[core] + low_core[...]
        low_part[core] = mine
        low_send[...] = mine.astype(bf16)
        for d in range(1, 4):
            c = remote(low_send, low_y.at[d - 1], sy_send.at[d - 1], sy_recv.at[d - 1], y_to[d - 1])
            c.start()
            sent.append(c)
        for d in range(1, 4):
            c = remote(vec.at[0], vec.at[d], sx_send.at[d - 1], sx_recv.at[d - 1], x_to[d - 1])
            c.start()
            sent.append(c)

    def send_low_back():
        total = low_part[core]
        for d in range(1, 4):
            sent[d].wait_recv()
            total = total + low_y[d - 1].astype(f32)
        low[core] = total.astype(bf16)
        c = remote(low.at[core], low.at[core], sc_send.at[1], sc_recv.at[1], other)
        c.start()
        sent.append(c)

    def early_gradient():
        sent[7].wait_recv()
        send_gradient(0)

    sent_z = []

    def send_gradient(n):
        hs = slice(0, 384) if n == 0 else slice(384, 512)
        grad = dot(low[0], mixed[:HALF, hs]) + dot(low[1], mixed[HALF:, hs])
        grads[0, :, hs] = (grad * LEN ** (-0.5)).astype(bf16)
        for d in range(7, 0, -1):
            at = 7 * n + d - 1
            c = remote(
                grads.at[0, :, pl.ds(384 * n, 128 if n else 384)],
                grads.at[d, :, pl.ds(384 * n, 128 if n else 384)],
                sz_send.at[at],
                sz_recv.at[at],
                z_to[d - 1],
            )
            c.start()
            sent_z.append(c)

    units = [(h, i) for h in range(HEADS) for i in range(2)]
    units += [(h, i) for h in range(HEADS) for i in range(2, BLOCKS)]
    events = [(12, project), (PLAN[0], send_low_core), (PLAN[1], send_low_y), (PLAN[2], send_low_back)]
    events.append((PLAN[3], early_gradient))
    done = 0
    for c in row_loads[:3]:
        c.wait()
    for c in chunks[1:]:
        c.start()
    held = None
    for h, i in units:
        ready = scores(h, i)
        if held is not None:
            mix(*held)
        held = (h, i, *ready)
        done += len(ready[1])
        while events and events[0][0] <= done:
            events.pop(0)[1]()
    mix(*held)

    send_gradient(1)
    for c in sent[4:7]:
        c.wait_recv()
    columns = jnp.concatenate([vec[d] for d in range(4)], axis=1)
    for c in sent_z:
        c.wait_recv()

    product = dot(grads[...].reshape(8 * RANK, COLS), columns)
    for n in range(4):
        whole[n] = product[:, 128 * n : 128 * (n + 1)]
    for half in range(2):
        for pair in range(8):
            rank = 8 * (pair // 2 % 2) + 4 * (pair // 4) + 2 * half + pair % 2
            for n in range(4):
                part[half, 8 * pair : 8 * pair + 8, 128 * n : 128 * (n + 1)] = whole[
                    n, pl.ds(rank, 8, stride=16), :
                ]
    c = remote(part.at[1 - core], part_core, sc_send.at[2], sc_recv.at[2], other)
    c.start()
    c.wait_recv()
    sent.append(c)
    part[core] = part[core] + part_core[...]
    rot_send[...] = part[core].reshape(4, 16, 512).astype(bf16)
    sent_y = []
    for d in range(1, 4):
        c = remote(
            rot_send.at[lax.rem(y + d, 4)], rot_y.at[d - 1], sy_send.at[2 + d], sy_recv.at[2 + d], y_to[d - 1]
        )
        c.start()
        sent_y.append(c)
    rotated = part[core, pl.ds(pl.multiple_of(16 * y, 16), 16), :]
    for d, c in enumerate(sent_y):
        c.wait_recv()
        rotated = rotated + rot_y[d].astype(f32)
    squares = rotated * rotated
    sums = []
    for half in (squares[:8], squares[8:]):
        for n in (4, 2, 1):
            half = half + pltpu.roll(half, n, 0)
        sums.append(half)
    pairs = jnp.where(lax.broadcasted_iota(jnp.int32, (8, COLS), 0) == 0, sums[0], sums[1])
    for d in range(4):
        spec_send[d] = pairs[:, 128 * d : 128 * (d + 1)]
    sent_x = []
    for d in range(1, 4):
        c = remote(spec_send.at[d], spec_x.at[d - 1], sx_send.at[2 + d], sx_recv.at[2 + d], x_from[d - 1])
        c.start()
        sent_x.append(c)
    total = spec_send[0]
    for d, c in enumerate(sent_x):
        c.wait_recv()
        total = total + spec_x[d]
    out_ref[...] = total[:2] * (1.0 / SEQS)
    for c in sent + sent_z + sent_y + sent_x:
        c.wait_send()


PLAN = (14, 30, 92, 110)


def shards(queries, keys, values, documents, cotangent, up, vectors):
    vmem = pltpu.VMEM
    dma = pltpu.SemaphoreType.DMA
    summed = pl.pallas_call(
        kernel,
        out_shape=jax.ShapeDtypeStruct((2, 128), f32),
        in_specs=[pl.BlockSpec(memory_space=pl.ANY)] * 7,
        out_specs=pl.BlockSpec(memory_space=pltpu.VMEM),
        scratch_shapes=[
            vmem((LEN, COLS), bf16),
            vmem((LEN, COLS), bf16),
            vmem((LEN, COLS), bf16),
            vmem((1, LEN), jnp.int32),
            vmem((LEN, FEATURES), bf16),
            vmem((RANK, FEATURES), bf16),
            vmem((4, COLS, 128), bf16),
            vmem((LEN, HEAD_DIM), bf16),
            vmem((LEN, HEAD_DIM), bf16),
            vmem((4, 128, 128), f32),
            vmem((LEN, COLS), bf16),
            vmem((2, RANK, HALF), f32),
            vmem((RANK, HALF), f32),
            vmem((RANK, HALF), bf16),
            vmem((3, RANK, HALF), bf16),
            vmem((2, RANK, HALF), bf16),
            vmem((8, RANK, COLS), bf16),
            vmem((2, 64, 512), f32),
            vmem((64, 512), f32),
            vmem((4, 16, 512), bf16),
            vmem((3, 16, 512), bf16),
            vmem((4, 8, 128), f32),
            vmem((3, 8, 128), f32),
            dma((3,)),
            dma((4,)),
            dma((6,)),
            dma((3,)),
            dma((3,)),
            dma((6,)),
            dma((6,)),
            dma((6,)),
            dma((6,)),
            dma((14,)),
            dma((14,)),
        ],
        compiler_params=pltpu.CompilerParams(
            collective_id=0, has_side_effects=True, vmem_limit_bytes=56 * 2**20
        ),
    )(queries, keys, values, documents, cotangent, up.T, vectors)
    return summed


def solution(mesh):
    return jax.shard_map(
        shards,
        mesh=mesh,
        in_specs=(
            P("dp", None, ("eig", "tensor")),
            P("dp", None, ("eig", "tensor")),
            P("dp", None, ("eig", "tensor")),
            P("dp", None),
            P("dp", None, ("eig", "tensor")),
            P(("eig", "tensor"), None),
            P(("eig", "tensor"), "dp"),
        ),
        out_specs=P(("eig", "tensor"), "dp"),
        check_vma=False,
    )
```

```python
import math

import jax
import jax.numpy as jnp
from jax import lax
from jax.experimental import pallas as pl
from jax.experimental.pallas import tpu as pltpu
from jax.sharding import PartitionSpec as P

HEAD_DIM = 128
HEADS = 4
LEN = 2048
RANK = 16
COLS = HEADS * HEAD_DIM
FEATURES = 1024
SEQS = 32
WINDOW = 1024
BLOCK = 256
BLOCKS = LEN // BLOCK
SCALE = math.log2(math.e) / math.sqrt(HEAD_DIM)
HALF = LEN // 2
NEG = -1e30
MESH = pl.DeviceIdType.MESH
f32 = jnp.float32
bf16 = jnp.bfloat16


def dot(a, b, ca=1, cb=0):
    return lax.dot_general(a, b, (((ca,), (cb,)), ((), ())), preferred_element_type=f32)


def places():
    dp = lax.axis_index("dp")
    eig = lax.axis_index("eig")
    tensor = lax.axis_index("tensor")
    return dp // 4, lax.rem(dp, 4), 2 * (tensor // 2) + eig, lax.rem(tensor, 2)


def device(z, x, y, core):
    return {"dp": 4 * z + x, "eig": lax.rem(y, 2), "tensor": 2 * (y // 2) + core}


def kernel(
    q_hbm, k_hbm, v_hbm, doc_hbm, cot_hbm, up_hbm, vec_hbm, out_ref,
    q, k, v, doc, cot, up, vec, kx, qx, whole, mixed,
    low_part, low_core, low_send, low_y, low,
    grads, part, part_core, rot_send, rot_y, spec_send, spec_x,
    in_sem, cot_sem, row_sem, sc_send, sc_recv, sy_send, sy_recv, sx_send, sx_recv, sz_send, sz_recv,
):
    z, x, y, core = places()
    other = device(z, x, y, 1 - core)
    y_to = [device(z, x, lax.rem(y + d, 4), core) for d in range(1, 4)]
    x_to = [device(z, lax.rem(x + d, 4), y, core) for d in range(1, 4)]
    x_from = [device(z, lax.rem(x + 4 - d, 4), y, core) for d in range(1, 4)]
    z_to = [device(lax.rem(z + d, 8), x, y, core) for d in range(1, 8)]
    peers = [other] + y_to + x_to + z_to

    def remote(src, dst, send, recv, to):
        return pltpu.make_async_remote_copy(
            src_ref=src, dst_ref=dst, send_sem=send, recv_sem=recv, device_id=to, device_id_type=MESH
        )

    loads = [
        pltpu.make_async_copy(src, dst, in_sem.at[n])
        for n, (src, dst) in enumerate([(doc_hbm, doc), (vec_hbm, vec.at[0]), (up_hbm, up)])
    ]
    row_loads = []
    for n in range(2):
        at = pl.ds(512 if n else 0, 1536 if n else 512)
        for m, (src, dst) in enumerate([(k_hbm, k), (q_hbm, q), (v_hbm, v)]):
            row_loads.append(pltpu.make_async_copy(src.at[0, at, :], dst.at[at, :], row_sem.at[3 * n + m]))
    chunks = [
        pltpu.make_async_copy(
            cot_hbm.at[0, pl.ds(512 * c, 512), :], cot.at[pl.ds(512 * c, 512), :], cot_sem.at[c]
        )
        for c in range(4)
    ]
    for c in row_loads[:3] + loads + chunks[:1]:
        c.start()
    barrier = pltpu.get_barrier_semaphore()
    for peer in peers:
        pl.semaphore_signal(barrier, inc=1, device_id=peer, device_id_type=MESH)

    loads[0].wait()
    one_hot = jnp.where(
        lax.broadcasted_iota(jnp.int32, (HEAD_DIM, LEN), 0) == doc[...], 1.0, 0.0
    ).astype(f32)
    turned = one_hot.T
    kx[...] = turned.astype(bf16)
    qx[...] = jnp.where(turned > 0.5, 0.0, NEG).astype(bf16)
    lower = lax.broadcasted_iota(jnp.int32, (BLOCK, BLOCK), 1) <= lax.broadcasted_iota(
        jnp.int32, (BLOCK, BLOCK), 0
    )
    ones = jnp.ones((BLOCK, HEAD_DIM), bf16)

    def scores(h, i):
        hs = slice(h * HEAD_DIM, (h + 1) * HEAD_DIM)
        rows = slice(i * BLOCK, (i + 1) * BLOCK)
        first = max(0, (i * BLOCK - WINDOW + 1) // BLOCK)
        query = jnp.concatenate([q[rows, hs], qx[rows, :]], axis=1)
        result = []
        for j in range(first, i + 1):
            at = slice(j * BLOCK, (j + 1) * BLOCK)
            key = jnp.concatenate([k[at, hs], kx[at, :]], axis=1)
            s = dot(query, key, 1, 1)
            result.append(jnp.where(lower, s, NEG) if j == i else s)
        return first, result

    def mix(h, i, first, blocks):
        hs = slice(h * HEAD_DIM, (h + 1) * HEAD_DIM)
        top = blocks[0]
        for s in blocks[1:]:
            top = jnp.maximum(top, s)
        top = jnp.max(top, axis=1, keepdims=True)
        total = None
        for n, s in enumerate(blocks):
            at = slice((first + n) * BLOCK, (first + n + 1) * BLOCK)
            weights = jnp.exp2((s - top) * SCALE).astype(bf16)
            term = dot(weights, jnp.concatenate([v[at, hs], ones], axis=1))
            total = term if total is None else total + term
        mixed[i * BLOCK : (i + 1) * BLOCK, hs] = (
            total[:, :HEAD_DIM] / total[:, HEAD_DIM:]
        ).astype(bf16)

    sent = []

    def project():
        loads[2].wait()
        for c in range(4):
            chunks[c].wait()
            if c == 0:
                for load in row_loads[3:]:
                    load.start()
            low_part[c // 2, :, pl.ds(512 * (c % 2), 512)] = dot(
                up[...], cot[512 * c : 512 * (c + 1), :], 1, 1
            )
        loads[1].wait()
        for c in row_loads[3:]:
            c.wait()

    def send_low_core():
        pl.semaphore_wait(barrier, len(peers))
        c = remote(low_part.at[1 - core], low_core, sc_send.at[0], sc_recv.at[0], other)
        c.start()
        sent.append(c)

    def send_low_y():
        sent[0].wait_recv()
        mine = low_part[core] + low_core[...]
        low_part[core] = mine
        low_send[...] = mine.astype(bf16)
        for d in range(1, 4):
            c = remote(low_send, low_y.at[d - 1], sy_send.at[d - 1], sy_recv.at[d - 1], y_to[d - 1])
            c.start()
            sent.append(c)
        for d in range(1, 4):
            c = remote(vec.at[0], vec.at[d], sx_send.at[d - 1], sx_recv.at[d - 1], x_to[d - 1])
            c.start()
            sent.append(c)

    def send_low_back():
        total = low_part[core]
        for d in range(1, 4):
            sent[d].wait_recv()
            total = total + low_y[d - 1].astype(f32)
        low[core] = total.astype(bf16)
        c = remote(low.at[core], low.at[core], sc_send.at[1], sc_recv.at[1], other)
        c.start()
        sent.append(c)

    def early_gradient():
        sent[7].wait_recv()
        send_gradient(0)

    sent_z = []

    def send_gradient(n):
        hs = slice(0, 384) if n == 0 else slice(384, 512)
        grad = dot(low[0], mixed[:HALF, hs]) + dot(low[1], mixed[HALF:, hs])
        grads[0, :, hs] = (grad * LEN ** (-0.5)).astype(bf16)
        for d in (4, 3, 5, 2, 6, 1, 7):
            at = 7 * n + d - 1
            c = remote(
                grads.at[0, :, pl.ds(384 * n, 128 if n else 384)],
                grads.at[d, :, pl.ds(384 * n, 128 if n else 384)],
                sz_send.at[at],
                sz_recv.at[at],
                z_to[d - 1],
            )
            c.start()
            sent_z.append(c)

    units = [(h, i) for h in range(HEADS) for i in range(2)]
    units += [(h, i) for h in range(HEADS) for i in range(2, BLOCKS)]
    events = [(12, project), (PLAN[0], send_low_core), (PLAN[1], send_low_y), (PLAN[2], send_low_back)]
    events.append((PLAN[3], early_gradient))
    done = 0
    for c in row_loads[:3]:
        c.wait()
    for c in chunks[1:]:
        c.start()
    held = None
    for h, i in units:
        ready = scores(h, i)
        if held is not None:
            mix(*held)
        held = (h, i, *ready)
        done += len(ready[1])
        while events and events[0][0] <= done:
            events.pop(0)[1]()
    mix(*held)

    send_gradient(1)
    for c in sent[4:7]:
        c.wait_recv()
    columns = jnp.concatenate([vec[d] for d in range(4)], axis=1)
    for c in sent_z[:7]:
        c.wait_recv()
    product = dot(grads[:, :, :384].reshape(8 * RANK, 384), columns[:384])
    for c in sent_z[7:]:
        c.wait_recv()

    product = product + dot(grads[:, :, 384:].reshape(8 * RANK, 128), columns[384:])
    for n in range(4):
        whole[n] = product[:, 128 * n : 128 * (n + 1)]
    for half in range(2):
        for pair in range(8):
            rank = 8 * (pair // 2 % 2) + 4 * (pair // 4) + 2 * half + pair % 2
            for n in range(4):
                part[half, 8 * pair : 8 * pair + 8, 128 * n : 128 * (n + 1)] = whole[
                    n, pl.ds(rank, 8, stride=16), :
                ]
    c = remote(part.at[1 - core], part_core, sc_send.at[2], sc_recv.at[2], other)
    c.start()
    c.wait_recv()
    sent.append(c)
    part[core] = part[core] + part_core[...]
    rot_send[...] = part[core].reshape(4, 16, 512).astype(bf16)
    sent_y = []
    for d in range(1, 4):
        c = remote(
            rot_send.at[lax.rem(y + d, 4)], rot_y.at[d - 1], sy_send.at[2 + d], sy_recv.at[2 + d], y_to[d - 1]
        )
        c.start()
        sent_y.append(c)
    rotated = part[core, pl.ds(pl.multiple_of(16 * y, 16), 16), :]
    for d, c in enumerate(sent_y):
        c.wait_recv()
        rotated = rotated + rot_y[d].astype(f32)
    squares = rotated * rotated
    sums = []
    for half in (squares[:8], squares[8:]):
        for n in (4, 2, 1):
            half = half + pltpu.roll(half, n, 0)
        sums.append(half)
    pairs = jnp.where(lax.broadcasted_iota(jnp.int32, (8, COLS), 0) == 0, sums[0], sums[1])
    for d in range(4):
        spec_send[d] = pairs[:, 128 * d : 128 * (d + 1)]
    sent_x = []
    for d in range(1, 4):
        c = remote(spec_send.at[d], spec_x.at[d - 1], sx_send.at[2 + d], sx_recv.at[2 + d], x_from[d - 1])
        c.start()
        sent_x.append(c)
    total = spec_send[0]
    for d, c in enumerate(sent_x):
        c.wait_recv()
        total = total + spec_x[d]
    out_ref[...] = total[:2] * (1.0 / SEQS)
    for c in sent + sent_z + sent_y + sent_x:
        c.wait_send()


PLAN = (14, 30, 92, 110)


def shards(queries, keys, values, documents, cotangent, up, vectors):
    vmem = pltpu.VMEM
    dma = pltpu.SemaphoreType.DMA
    summed = pl.pallas_call(
        kernel,
        out_shape=jax.ShapeDtypeStruct((2, 128), f32),
        in_specs=[pl.BlockSpec(memory_space=pl.ANY)] * 7,
        out_specs=pl.BlockSpec(memory_space=pltpu.VMEM),
        scratch_shapes=[
            vmem((LEN, COLS), bf16),
            vmem((LEN, COLS), bf16),
            vmem((LEN, COLS), bf16),
            vmem((1, LEN), jnp.int32),
            vmem((LEN, FEATURES), bf16),
            vmem((RANK, FEATURES), bf16),
            vmem((4, COLS, 128), bf16),
            vmem((LEN, HEAD_DIM), bf16),
            vmem((LEN, HEAD_DIM), bf16),
            vmem((4, 128, 128), f32),
            vmem((LEN, COLS), bf16),
            vmem((2, RANK, HALF), f32),
            vmem((RANK, HALF), f32),
            vmem((RANK, HALF), bf16),
            vmem((3, RANK, HALF), bf16),
            vmem((2, RANK, HALF), bf16),
            vmem((8, RANK, COLS), bf16),
            vmem((2, 64, 512), f32),
            vmem((64, 512), f32),
            vmem((4, 16, 512), bf16),
            vmem((3, 16, 512), bf16),
            vmem((4, 8, 128), f32),
            vmem((3, 8, 128), f32),
            dma((3,)),
            dma((4,)),
            dma((6,)),
            dma((3,)),
            dma((3,)),
            dma((6,)),
            dma((6,)),
            dma((6,)),
            dma((6,)),
            dma((14,)),
            dma((14,)),
        ],
        compiler_params=pltpu.CompilerParams(
            collective_id=0, has_side_effects=True, vmem_limit_bytes=56 * 2**20
        ),
    )(queries, keys, values, documents, cotangent, up.T, vectors)
    return summed


def solution(mesh):
    return jax.shard_map(
        shards,
        mesh=mesh,
        in_specs=(
            P("dp", None, ("eig", "tensor")),
            P("dp", None, ("eig", "tensor")),
            P("dp", None, ("eig", "tensor")),
            P("dp", None),
            P("dp", None, ("eig", "tensor")),
            P(("eig", "tensor"), None),
            P(("eig", "tensor"), "dp"),
        ),
        out_specs=P(("eig", "tensor"), "dp"),
        check_vma=False,
    )
```
